512 devices in a mesh: ctx: 32 (over z, core), exp: 16 (over y, x).
Axes of the slice: x: 4, y: 4, z: 16, core: 2. Of those that a mesh axis runs over, the one named last changes fastest.
Arguments:
- ssm_input: bfloat16 [4096, 8192], P('ctx', 'exp'), may hold values from -6 to 6
- gate_input: bfloat16 [4096, 8192], P('ctx', 'exp'), may hold values from -6 to 6
- state_in_proj: bfloat16 [4096, 128], P('ctx'), may hold values from -0.29882812 to 0.29882812
- state_out_proj: bfloat16 [4096, 128], P('ctx'), may hold values from -0.5 to 0.5
- log_decay: float32 [4096, 128], P('ctx', 'exp'), as said below
- skip_gain: float32 [128], P('exp'), may hold values from 0.5 to 1.5
- out_weight: bfloat16 [8192, 4096], P('exp', 'ctx'), may hold values from -0.0625 to 0.0625
- routes: int32 [4096, 2], replicated, may hold values from 0 to 15, all different within a row; in each aligned block of 8 rows (0 to 7, 8 to 15, ...) at most 2 rows name the same one
- route_weights: bfloat16 [4096, 2], replicated, may hold values from 0.099609375 to 1
- expert_gate: bfloat16 [16, 4096, 12288], P('exp', None, 'ctx'), may hold values from -0.09375 to 0.09375
Outputs:
- gate_act: bfloat16 [16, 1024, 12288], P('exp', None, 'ctx')
The draws below stay inside these ranges and needn't reach their ends.
Inputs may be any that keep to these rules, and one draw needn't show every extreme that they name: `routes`: each row names 2 different experts, every expert is named by some row, and in each aligned block of 8 rows no expert is named by more than 2 rows. `log_decay`: every entry is negative.
All inputs are finite; a program needn't handle non-finite values.
Results may differ from the reference program's by a relative error of at most 0.025.
Values may be sent and summed in bfloat16 or wider, within the bound.
A program may use at most 128 MiB of HBM per device.

```python
import math
import jax
import jax.numpy as jnp
import numpy as np
from jax import lax

D = 4096
SCAN_HEADS = 128
STATE = 128
FF = 12288
TOPK = 2
TOK_CTX = 128
SEQUENCE_TOKENS = 4096
INNER = 8192
EXPERTS = 16
CAP = 2
N_EXP = 16


def draw_log_decay(key, part):
    key = jax.random.fold_in(key, 11)
    random_subkeys = jax.random.split(key, 7)
    slow_share = 0.5
    slow_heads = jax.random.uniform(random_subkeys[0], (SCAN_HEADS,)) < slow_share
    slow_rate = jax.random.uniform(random_subkeys[1], (SCAN_HEADS,), minval=0.2, maxval=0.6) / SEQUENCE_TOKENS
    fast_rate = jax.random.uniform(random_subkeys[2], (SCAN_HEADS,), minval=0.04, maxval=0.07)
    decay_speed = jnp.where(slow_heads, slow_rate, fast_rate)
    block_factor = jnp.exp(jax.random.uniform(random_subkeys[3], (SEQUENCE_TOKENS // 16, SCAN_HEADS), minval=-0.7, maxval=0.7))
    token_factor = jnp.exp(jax.random.uniform(random_subkeys[4], (SEQUENCE_TOKENS, SCAN_HEADS), minval=-0.3, maxval=0.3))
    multiplier = jnp.repeat(block_factor, 16, axis=0) * token_factor
    spike_position = jax.random.randint(random_subkeys[5], (3,), 0, SEQUENCE_TOKENS)
    spike_events = jnp.any(jnp.arange(SEQUENCE_TOKENS)[:, None] == spike_position[None, :], axis=1)
    spike_magnitude = jax.random.uniform(random_subkeys[6], (SCAN_HEADS,), minval=0.22, maxval=0.5)
    value_entries = -(decay_speed[None, :] * multiplier) - jnp.where(spike_events[:, None], spike_magnitude[None, :], 0.0)
    return value_entries.astype(jnp.float32)


def block_levels(key, dims, cuts, least, largest):
    gain, own = 1.0, jax.random.fold_in(key, 6)
    for dim, parts in cuts:
        steps = jnp.exp(jax.random.uniform(jax.random.fold_in(own, dim), (parts,), jnp.float32, least / len(cuts), largest / len(cuts)))
        gain = gain * jnp.repeat(steps, dims[dim] // parts).reshape([-1 if axis == dim else 1 for axis in range(len(dims))])
    return gain


def routed_block(stream_key, own, number, rows, amount, top, reach, lean):
    ranking = jax.random.permutation(stream_key, amount)
    packed, usual = portions_of(amount, rows * top, reach, lean, True), portions_of(amount, rows * top, reach, lean, False)
    places = jnp.arange(amount)

    def named(sizes, offset_by):
        used = int((sizes > 0).sum())
        fixed = max(1, used // 4)
        passed = fixed + (places - fixed + offset_by * (used - fixed)) % max(1, amount - fixed)
        return jnp.zeros((amount,), jnp.int32).at[ranking[jnp.where(places < fixed, places, passed)]].set(jnp.asarray(sizes, jnp.int32))

    sizes = jnp.where(number % 4 == 0, named(packed, number // 4), named(usual, number - number // 4 - 1))
    mixed = jax.random.permutation(jax.random.fold_in(own, 3), amount)
    source_of, receiver = mixed[0:amount // 2 * 2:2], mixed[1:amount // 2 * 2:2]
    room = jnp.minimum(sizes[source_of] - 1, reach - sizes[receiver]) // 2
    room = jnp.where((source_of == ranking[0]) | (receiver == ranking[0]) | (sizes[receiver] == 0), 0, jnp.maximum(room, 0))
    passed = jax.random.randint(jax.random.fold_in(own, 4), (amount // 2,), 0, 1 << 20) % (room + 1)
    sizes = sizes.at[source_of].add(-passed).at[receiver].add(passed)
    members = jnp.searchsorted(jnp.cumsum(sizes), jnp.arange(rows * top), side="right").astype(jnp.int32)
    grid = members.reshape(top, rows).T
    grid = grid[jax.random.permutation(jax.random.fold_in(own, 1), rows)]
    offset_by = jax.random.randint(jax.random.fold_in(own, 2), (rows, 1), 0, top)
    return jnp.take_along_axis(grid, (jnp.arange(top)[None, :] + offset_by) % top, axis=1)


def portions_of(number_of, total, limit, lean, full):
    weights = [(1 << 20) // math.isqrt(rank ** lean) + 1 for rank in range(1, number_of + 1)]
    largest = limit if full else min(limit, max(-(-total // number_of), total * weights[0] // sum(weights)))
    least = 1 if total - largest >= number_of - 1 else 0
    given, spare = [largest] + [least] * (number_of - 1), total - largest - least * (number_of - 1)
    while spare > 0:
        free = [i for i in range(1, number_of) if given[i] < largest] or [i for i in range(1, number_of) if given[i] < limit]
        whole, left = sum([weights[i] for i in free]), spare
        for i in free:
            addition = min(limit - given[i], max(1, left * weights[i] // whole), spare)
            given[i] = given[i] + addition
            spare = spare - addition
    return np.array(given)


def normal_values(own_key, shape, deviation, reach, shards=(), held_as=jnp.bfloat16):
    result = jax.random.normal(own_key, shape, jnp.float32) * deviation
    if len(shards) > 0:
        result = block_levels(own_key, shape, shards, -0.22, 0.18) * result
    return jnp.clip(result, min=-reach, max=reach).astype(held_as)


def setup_inputs(seed: int = 0) -> dict:
    key_list = jax.random.split(jax.random.key(seed), 11)
    ssm_input = normal_values(key_list[0], (SEQUENCE_TOKENS, INNER), 1.0, 6.0, ((0, 32), (1, 16)))
    gate_input = normal_values(key_list[1], (SEQUENCE_TOKENS, INNER), 1.0, 6.0, ((0, 32), (1, 16)))
    state_in_proj = normal_values(key_list[2], (SEQUENCE_TOKENS, STATE), 0.05, 0.29882812, ((0, 32),))
    state_out_proj = normal_values(key_list[3], (SEQUENCE_TOKENS, STATE), STATE ** -0.5, 0.5, ((0, 32),))
    log_decay = draw_log_decay(jax.random.fold_in(key_list[10], 71), 0)
    skip_gain = jnp.clip(0.5 + 1.0 * jax.random.uniform(key_list[5], (SCAN_HEADS,), jnp.float32) ** block_levels(key_list[5], (SCAN_HEADS,), ((0, 16),), -0.2, 0.2), 0.5, 1.5)
    out_weight = normal_values(key_list[6], (INNER, D), INNER ** -0.5, 0.0625, ((0, 16), (1, 32)))
    routes_keys = jax.random.split(jax.random.fold_in(key_list[7], 1), SEQUENCE_TOKENS // (TOK_CTX // N_EXP))
    routes_turns = jax.random.permutation(jax.random.fold_in(key_list[7], 3), SEQUENCE_TOKENS // (TOK_CTX // N_EXP))
    routes = jax.vmap(lambda own, number: routed_block(jax.random.fold_in(key_list[7], 2), own, number, TOK_CTX // N_EXP, EXPERTS, TOPK, CAP, 2))(routes_keys, routes_turns).reshape((SEQUENCE_TOKENS, TOPK))
    route_weights = jnp.clip(jax.random.uniform(key_list[8], (SEQUENCE_TOKENS, TOPK), jnp.float32, 0.099609375, 1.0), 0.099609375, 1.0).astype(jnp.bfloat16)
    expert_gate = normal_values(key_list[9], (EXPERTS, D, FF), D ** -0.5, 0.09375, ((0, 16), (2, 32)))
    return {"ssm_input": ssm_input, "gate_input": gate_input, "state_in_proj": state_in_proj, "state_out_proj": state_out_proj, "log_decay": log_decay, "skip_gain": skip_gain, "out_weight": out_weight, "routes": routes, "route_weights": route_weights, "expert_gate": expert_gate}


def reference(ssm_input, gate_input, state_in_proj, state_out_proj, log_decay, skip_gain, out_weight, routes, route_weights, expert_gate):
    highest = lax.Precision.HIGHEST
    seq_len = ssm_input.shape[0]
    head_count = log_decay.shape[1]
    head_width = ssm_input.shape[1] // head_count
    inputs = ssm_input.astype(jnp.float32).reshape(seq_len, head_count, head_width)
    state_map = state_in_proj.astype(jnp.float32)
    read_map = state_out_proj.astype(jnp.float32)
    decays = jnp.exp(log_decay)

    def advance(carry_state, items):
        step_input, step_map, step_read, step_decay = items
        carry_state = step_decay[:, None, None] * carry_state + step_input[:, :, None] * step_map[None, None, :]
        return carry_state, jnp.einsum("hpn,n->hp", carry_state, step_read, precision=highest)

    initial = jnp.zeros((head_count, head_width, state_map.shape[1]), jnp.float32)
    final_state, outputs = lax.scan(advance, initial, (inputs, state_map, read_map, decays))
    outputs = outputs + skip_gain[None, :, None] * inputs
    gated_out = (outputs.reshape(seq_len, -1) * jax.nn.silu(gate_input.astype(jnp.float32))).astype(jnp.bfloat16)
    group_width = gated_out.shape[1] // N_EXP
    summed = jnp.zeros((seq_len, out_weight.shape[1]), jnp.float32)
    for group_index in range(N_EXP):
        lower = group_index * group_width
        partial_value = jnp.dot(gated_out[:, lower:lower + group_width], out_weight[lower:lower + group_width], preferred_element_type=jnp.float32)
        rounded = lax.optimization_barrier(partial_value.astype(jnp.bfloat16))
        summed = summed + rounded.astype(jnp.float32)
    mixed_rows = summed.astype(jnp.bfloat16)
    block_rows = TOK_CTX // N_EXP
    sources = seq_len // block_rows
    route_ids = routes.reshape(sources, block_rows * TOPK)
    onehot = (route_ids[:, :, None] == jnp.arange(EXPERTS, dtype=jnp.int32)[None, None, :]).astype(jnp.int32)
    before = jnp.cumsum(onehot, axis=1) - onehot
    slot_pos = jnp.sum(before * onehot, axis=2)
    row_index = (jnp.arange(sources, dtype=jnp.int32)[:, None] * CAP + slot_pos).reshape(-1).astype(jnp.int32)
    expert_of = route_ids.reshape(-1).astype(jnp.int32)
    token_of = (jnp.arange(seq_len * TOPK, dtype=jnp.int32) // TOPK).astype(jnp.int32)
    expert_rows = jnp.zeros((EXPERTS, sources * CAP, D), jnp.bfloat16).at[expert_of, row_index].set(mixed_rows[token_of])
    slot_weight = jnp.zeros((EXPERTS, sources * CAP), jnp.float32).at[expert_of, row_index].set(route_weights.reshape(-1).astype(jnp.float32))

    def per_expert(items):
        rows_here, weights_here, gate_here = items
        product = jnp.dot(rows_here, gate_here, preferred_element_type=jnp.float32)
        return (weights_here[:, None] * jax.nn.silu(product)).astype(jnp.bfloat16)

    return lax.map(per_expert, (expert_rows, slot_weight, expert_gate))
```

```python
import jax
import jax.numpy as jnp
from jax import lax
from jax.experimental import pallas as pl
from jax.experimental.pallas import tpu as pltpu
from jax.sharding import PartitionSpec as P

MESH = pl.DeviceIdType.MESH
SOURCE = 8
CAP = 2
FLOOR = -110.0
HIGHEST = lax.Precision.HIGHEST
WQ = 4
AQ = 2
bf16 = jnp.bfloat16
f32 = jnp.float32


def dot(a, b, dims=((1,), (0,)), precision=None):
    return lax.dot_general(a, b, (dims, ((), ())), preferred_element_type=f32, precision=precision)


def iota(shape, dim):
    return lax.broadcasted_iota(jnp.int32, shape, dim)


def silu(v):
    return v / (1.0 + jnp.exp(-v))


def kernel(
    x_ref, gt_ref, b_ref, c_ref, ld_ref, skip_ref, w_hbm, r_ref, rw_ref, g_hbm,
    out_ref,
    wbuf, abuf, gbuf, psend, precv, dsend, stb, dec, rs, rd, pre, carr,
    g_sem, w_sem, s1_send, s1_recv, d1_send, d1_recv, s2_send, s2_recv,
    w_send, w_recv, ws_send, ws_recv, p_send, p_recv, m_send, m_recv, a_send, a_recv, as_send, as_recv,
):
    nc, ne = lax.axis_size("ctx"), lax.axis_size("exp")
    nz = nc // 2
    up, down = nz // 2, nz - 1 - nz // 2
    c, e = lax.axis_index("ctx"), lax.axis_index("exp")
    z, core = c // 2, c % 2
    tokens, width = x_ref.shape
    heads = ld_ref.shape[1]
    hw = width // heads
    cols = psend.shape[2]

    def at_z(chip, lane):
        return {"ctx": lax.rem(chip + nz, nz) * 2 + lane}

    barrier = pltpu.get_barrier_semaphore()
    for k in range(1, nc):
        pl.semaphore_signal(barrier, 1, device_id={"ctx": lax.rem(c + k, nc)}, device_id_type=MESH)
    for k in range(1, ne):
        pl.semaphore_signal(barrier, 1, device_id={"exp": lax.rem(e + k, ne)}, device_id_type=MESH)

    load_g = pltpu.make_async_copy(g_hbm.at[0], gbuf, g_sem)
    load_w = pltpu.make_async_copy(w_hbm, wbuf.at[c], w_sem)
    load_w.start()
    load_g.start()

    ld = jnp.maximum(ld_ref[...], FLOOR)
    row, col = iota((tokens, tokens), 0), iota((tokens, tokens), 1)
    causal = row >= col
    cum = dot(causal.astype(f32), ld, precision=HIGHEST)
    cum_t = dot(ld, (row <= col).astype(f32), ((0,), (0,)), HIGHEST)
    spread = (iota((heads, width), 1) // hw == iota((heads, width), 0)).astype(f32)
    cum_x = dot(cum, spread, precision=HIGHEST)
    x = x_ref[...]
    xf = x.astype(f32)
    span = jnp.exp(cum_x[tokens - 1 :, :])
    to_end = jnp.exp(cum_x[tokens - 1 :, :] - cum_x)
    local = dot(b_ref[...], (xf * to_end).astype(bf16), ((0,), (0,))).astype(bf16)
    lane_blocks = width // 128
    for j in range(nc):
        rb, lb = j // lane_blocks, j % lane_blocks
        stb[j] = local[rb * 16 : (rb + 1) * 16, lb * 128 : (lb + 1) * 128]
    for lb in range(lane_blocks):
        dec[lb] = span[:, lb * 128 : (lb + 1) * 128]

    pl.semaphore_wait(barrier, nc - 1 + ne - 1)

    def s1(j):
        return pltpu.make_async_remote_copy(
            stb.at[j], rs.at[c], s1_send, s1_recv, device_id={"ctx": j}, device_id_type=MESH)

    def d1(j):
        return pltpu.make_async_remote_copy(
            dec.at[lax.rem(j, lane_blocks)], rd.at[c], d1_send, d1_recv, device_id={"ctx": j}, device_id_type=MESH)

    def s2(j):
        place = carr.at[pl.ds(pl.multiple_of(c // lane_blocks * 16, 16), 16), pl.ds(pl.multiple_of(c % lane_blocks * 128, 128), 128)]
        return pltpu.make_async_remote_copy(
            pre.at[j], place, s2_send, s2_recv, device_id={"ctx": j}, device_id_type=MESH)

    def await_bytes(ref, sem):
        pltpu.make_async_copy(ref, ref, sem).wait()

    wrows = wbuf.shape[1] // WQ

    def w_piece(chip, lane, q):
        return wbuf.at[lax.rem(chip + nz, nz) * 2 + lane, pl.ds(q * wrows, wrows), :]

    def w_hop(dd, i, q):
        turn = 1 - 2 * dd
        piece = w_piece(z - turn * i, core, q)
        return pltpu.make_async_remote_copy(
            piece, piece, w_send, w_recv.at[dd, i, q], device_id=at_z(z + turn, core), device_id_type=MESH)

    def w_arrived(dd, i, q):
        piece = w_piece(z - (1 - 2 * dd) * (i + 1), core, q)
        pltpu.make_async_copy(piece, piece, w_recv.at[dd, i, q]).wait()

    def w_side(chip):
        chip = lax.rem(chip + nz, nz)
        block = wbuf.at[chip * 2 + core]
        return pltpu.make_async_remote_copy(
            block, block, ws_send, ws_recv.at[chip], device_id={"ctx": c + 1 - 2 * core}, device_id_type=MESH)

    def w_step(i):
        for q in range(WQ):
            for dd, hops in ((0, up), (1, down)):
                if 0 < i <= hops:
                    w_arrived(dd, i - 1, q)
                if i < hops:
                    w_hop(dd, i, q).start()
        if i == 0:
            w_side(z).start()
        else:
            for dd, hops in ((0, up), (1, down)):
                if i <= hops:
                    w_side(z - (1 - 2 * dd) * i).start()

    load_w.wait()
    for k in range(1, nc):
        s1(lax.rem(c + k, nc)).start()
        d1(lax.rem(c + k, nc)).start()
    w_step(0)
    rs[pl.ds(c, 1)] = stb[pl.ds(c, 1)]
    rd[pl.ds(c, 1)] = dec[pl.ds(lax.rem(c, lane_blocks), 1)]

    scores = dot(c_ref[...], b_ref[...], ((1,), (1,)))
    pairs = []
    for p in range(width // 128):
        xp = x[:, p * 128 : (p + 1) * 128]
        part = None
        for h in range(p * 128 // hw, (p + 1) * 128 // hw):
            gap = jnp.minimum(cum[:, h : h + 1] - cum_t[h : h + 1, :], 0.0)
            mixing = (jnp.where(causal, jnp.exp(gap), 0.0) * scores).astype(bf16)
            y = dot(mixing, xp)
            part = y if part is None else jnp.where(iota(y.shape, 1) // hw == h - p * 128 // hw, y, part)
        pairs.append(part)
    skip = dot(skip_ref[...], spread, precision=HIGHEST)
    within = jnp.concatenate(pairs, axis=1) + skip * xf

    same = (row // SOURCE == col // SOURCE) & (row < col)
    before = same.astype(bf16)
    r0, r1 = r_ref[0, pl.ds(c, 1), :], r_ref[1, pl.ds(c, 1), :]
    experts = iota((ne, tokens), 0)
    hit = (r0 == experts) | (r1 == experts)
    pos = dot(hit.astype(bf16), before)
    slots = tokens // SOURCE * CAP
    target = jnp.where(hit, (iota((ne, tokens), 1) // SOURCE) * CAP + pos.astype(jnp.int32), -1)
    masks = (target[:, None, :] == iota((ne, slots, tokens), 1)).astype(f32).astype(bf16).reshape(ne * slots, tokens)
    own0, own1 = (r_ref[0] == e), (r_ref[1] == e)
    own = own0 | own1
    own_pos = dot(own.astype(bf16), before)
    own_target = jnp.where(own, (iota((nc, tokens), 1) // SOURCE) * CAP + own_pos.astype(jnp.int32), -1)
    own_weight = jnp.where(own0, rw_ref[0], jnp.where(own1, rw_ref[1], 0.0))

    w_step(1)
    w_step(2)

    await_bytes(rs.at[pl.ds(0, nc - 1)], s1_recv)
    await_bytes(rd.at[pl.ds(0, nc - 1)], d1_recv)
    state = jnp.zeros(rs.shape[1:], f32)
    for j in range(nc):
        pre[j] = state.astype(bf16)
        state = rd[j] * state + rs[j].astype(f32)
    for k in range(1, nc):
        s2(lax.rem(c + k, nc)).start()
    carr[pl.ds(pl.multiple_of(c // lane_blocks * 16, 16), 16), pl.ds(pl.multiple_of(c % lane_blocks * 128, 128), 128)] = pre[c]

    w_step(3)
    w_step(4)

    await_bytes(pre.at[pl.ds(0, nc - 1)], s2_recv)
    from_before = dot(c_ref[...], carr[...]) * jnp.exp(cum_x)
    gated = ((within + from_before) * silu(gt_ref[...].astype(f32))).astype(bf16)

    for i in range(5, up + 1):
        w_step(i)
    for k in range(nz):
        block = wbuf.at[k * 2 + 1 - core]
        pltpu.make_async_copy(block, block, ws_recv.at[k]).wait()

    def p_copy(j):
        return pltpu.make_async_remote_copy(
            psend.at[j], precv.at[e], p_send, p_recv, device_id={"exp": j}, device_id_type=MESH)

    shards = cols // 128

    def project(k, _):
        j = lax.rem(e + k, ne)
        for s in range(shards):
            psend[j, :, s * 128 : (s + 1) * 128] = dot(gated, wbuf[j * shards + s]).astype(bf16)

        @pl.when(k < ne)
        def _():
            p_copy(j).start()

        return 0

    lax.fori_loop(1, ne + 1, project, 0)
    precv[pl.ds(e, 1)] = psend[pl.ds(e, 1)]
    await_bytes(psend.at[pl.ds(0, ne - 1)], p_recv)
    total = precv[0].astype(f32)
    for k in range(1, ne):
        total += precv[k].astype(f32)
    mixed = total.astype(bf16)

    def m_copy(j):
        return pltpu.make_async_remote_copy(
            dsend.at[j], abuf.at[c, :, pl.ds(pl.multiple_of(e * cols, cols), cols)], m_send, m_recv,
            device_id={"exp": j}, device_id_type=MESH)

    dsend[...] = dot(masks, mixed).astype(bf16).reshape(dsend.shape)
    for k in range(1, ne):
        m_copy(lax.rem(e + k, ne)).start()
    abuf[pl.ds(c, 1), :, pl.ds(pl.multiple_of(e * cols, cols), cols)] = dsend[pl.ds(e, 1)]
    load_g.wait()
    await_bytes(dsend.at[pl.ds(0, ne - 1)], m_recv)

    arows = abuf.shape[1] // AQ

    def a_piece(chip, lane, q):
        return abuf.at[lax.rem(chip + nz, nz) * 2 + lane, pl.ds(q * arows, arows), :]

    def a_hop(dd, i, q):
        turn = 1 - 2 * dd
        piece = a_piece(z - turn * i, core, q)
        return pltpu.make_async_remote_copy(
            piece, piece, a_send, a_recv.at[dd, i, q], device_id=at_z(z + turn, core), device_id_type=MESH)

    def a_arrived(dd, i, q):
        piece = a_piece(z - (1 - 2 * dd) * (i + 1), core, q)
        pltpu.make_async_copy(piece, piece, a_recv.at[dd, i, q]).wait()

    def a_side(chip):
        block = abuf.at[chip * 2 + core]
        return pltpu.make_async_remote_copy(
            block, block, as_send, as_recv.at[chip], device_id={"ctx": c + 1 - 2 * core}, device_id_type=MESH)

    own_target = own_target.astype(f32)

    def expert(chip):
        block = abuf.at[chip * 2 + 1 - core]
        pltpu.make_async_copy(block, block, as_recv.at[chip]).wait()
        rows = abuf[pl.ds(chip * 2, 2)].reshape(2 * slots, abuf.shape[2])
        product = dot(rows, gbuf[...])
        weights = []
        for k in range(2):
            pick = iota((nc, tokens), 0) == chip * 2 + k
            goal = jnp.sum(jnp.where(pick, own_target, 0.0), axis=0, keepdims=True)
            value = jnp.sum(jnp.where(pick, own_weight, 0.0), axis=0, keepdims=True)
            at = goal == iota((slots, tokens), 0).astype(f32)
            weights.append(jnp.sum(jnp.where(at, value, 0.0), axis=1, keepdims=True))
        weight = jnp.concatenate(weights, axis=0)
        out_ref[0, pl.ds(pl.multiple_of(chip * 2 * slots, 2 * slots), 2 * slots), :] = (weight * silu(product)).astype(bf16)

    def a_step(i, _):
        for q in range(AQ):
            for dd, hops in ((0, up), (1, down)):

                @pl.when((i > 0) & (i <= hops))
                def _():
                    a_arrived(dd, i - 1, q)

                @pl.when(i < hops)
                def _():
                    a_hop(dd, i, q).start()

        for dd, hops in ((0, up), (1, down)):

            @pl.when((i <= hops) & ((i > 0) | (dd == 0)))
            def _():
                a_side(lax.rem(z - (1 - 2 * dd) * i + nz, nz)).start()

        for dd, hops in ((0, up), (1, down)):

            @pl.when((i > 0) & (i <= hops + 1) & ((i > 1) | (dd == 0)))
            def _():
                expert(lax.rem(z - (1 - 2 * dd) * (i - 1) + nz, nz))

        return 0

    lax.fori_loop(0, up + 2, a_step, 0)

    await_bytes(stb.at[pl.ds(0, nc - 1)], s1_send)
    await_bytes(rd.at[pl.ds(0, nc - 1)], d1_send)
    await_bytes(pre.at[pl.ds(0, nc - 1)], s2_send)
    await_bytes(wbuf.at[pl.ds(0, nz - 1)], w_send)
    await_bytes(wbuf.at[pl.ds(0, nz)], ws_send)
    await_bytes(psend.at[pl.ds(0, ne - 1)], p_send)
    await_bytes(dsend.at[pl.ds(0, ne - 1)], m_send)
    await_bytes(abuf.at[pl.ds(0, nz - 1)], a_send)
    await_bytes(abuf.at[pl.ds(0, nz)], as_send)


def body(x, gt, b, c, ld, skip, w, routes, weights, gate):
    nc, ne = lax.axis_size("ctx"), lax.axis_size("exp")
    tokens, width = x.shape
    heads = ld.shape[1]
    depth, shard = w.shape
    wide = shard * nc
    cols = wide // ne
    slots = tokens // SOURCE * CAP
    ff = gate.shape[2]
    lane_blocks = width // 128
    r = routes.T.reshape(2, nc, tokens)
    rw = weights.astype(f32).T.reshape(2, nc, tokens)
    vmem = pl.BlockSpec(memory_space=pltpu.VMEM)
    hbm = pl.BlockSpec(memory_space=pl.ANY)
    dma = pltpu.SemaphoreType.DMA
    return pl.pallas_call(
        kernel,
        out_shape=jax.ShapeDtypeStruct((1, nc * slots, ff), bf16),
        in_specs=[vmem] * 6 + [hbm] + [vmem] * 2 + [hbm],
        out_specs=vmem,
        scratch_shapes=[
            pltpu.VMEM((nc, depth, shard), bf16),
            pltpu.VMEM((nc, slots, wide), bf16),
            pltpu.VMEM((wide, ff), bf16),
            pltpu.VMEM((ne, tokens, cols), bf16),
            pltpu.VMEM((ne, tokens, cols), bf16),
            pltpu.VMEM((ne, slots, cols), bf16),
            pltpu.VMEM((nc, 16, 128), bf16),
            pltpu.VMEM((lane_blocks, 1, 128), f32),
            pltpu.VMEM((nc, 16, 128), bf16),
            pltpu.VMEM((nc, 1, 128), f32),
            pltpu.VMEM((nc, 16, 128), bf16),
            pltpu.VMEM((b.shape[1], width), bf16),
            dma, dma,
            dma, dma, dma, dma, dma, dma,
            dma, dma((2, nc // 4, WQ)), dma, dma((nc // 2,)),
            dma, dma, dma, dma,
            dma, dma((2, nc // 4, AQ)), dma, dma((nc // 2,)),
        ],
        compiler_params=pltpu.CompilerParams(
            collective_id=0, has_side_effects=True, vmem_limit_bytes=48 * 2**20
        ),
        name="hybrid_block",
    )(x, gt, b, c, ld, skip.reshape(1, heads), w, r, rw, gate)


def solution(mesh):
    in_specs = (
        P("ctx", "exp"),
        P("ctx", "exp"),
        P("ctx", None),
        P("ctx", None),
        P("ctx", "exp"),
        P("exp"),
        P("exp", "ctx"),
        P(),
        P(),
        P("exp", None, "ctx"),
    )
    out_specs = P("exp", None, "ctx")
    return jax.shard_map(body, mesh=mesh, in_specs=in_specs, out_specs=out_specs, check_vma=False)
```

```python
import jax
import jax.numpy as jnp
from jax import lax
from jax.experimental import pallas as pl
from jax.experimental.pallas import tpu as pltpu
from jax.sharding import PartitionSpec as P

MESH = pl.DeviceIdType.MESH
SOURCE = 8
CAP = 2
FLOOR = -110.0
HIGHEST = lax.Precision.HIGHEST
WQ = 4
AQ = 4
NEAR = 5
LANES = 128
bf16 = jnp.bfloat16
f32 = jnp.float32


def dot(a, b, dims=((1,), (0,)), precision=None):
    return lax.dot_general(a, b, (dims, ((), ())), preferred_element_type=f32, precision=precision)


def iota(shape, dim):
    return lax.broadcasted_iota(jnp.int32, shape, dim)


def silu(v):
    return v / (1.0 + jnp.exp(-v))


def await_bytes(ref, sem):
    pltpu.make_async_copy(ref, ref, sem).wait()


def kernel(
    x_hbm, gt_hbm, b_hbm, c_hbm, ld_hbm, skip_hbm, w_hbm, r_hbm, rw_hbm, g_hbm,
    out_ref,
    x_ref, gt_ref, b_ref, c_ref, ld_ref, skip_ref, r_ref, rw_ref, gbuf, wbuf, abuf, bbuf, psend, precv, dsend, bsend, mbuf,
    gall, lst, lsib, span, span_sib, stb, dec, rs, rd, pre, ent, goal_ref, value_ref,
    l_sem, l_send, l_recv, s1_send, s1_recv, d1_send, d1_recv, s2_send, s2_recv, e_send, e_recv,
    w_send, w_recv, g_send, g_recv, p_send, p_recv, m_send, m_recv, a_send, a_recv, as_send, as_recv,
    b_send, b_recv, bd_send, bd_recv, bs_send, bs_recv,
):
    nc, ne = lax.axis_size("ctx"), lax.axis_size("exp")
    nz = nc // 2
    up = nz // 2
    c, e = lax.axis_index("ctx"), lax.axis_index("exp")
    z, core = c // 2, c % 2
    tokens, width = x_ref.shape
    heads = ld_ref.shape[0]
    hw = width // heads
    half = width // 2
    slots = tokens // SOURCE * CAP
    sibling = {"ctx": c + 1 - 2 * core}

    def ring(chip):
        return lax.rem(chip + nz, nz)

    def at_z(chip):
        return {"ctx": ring(chip) * 2 + core}

    def remote(src, dst, send, recv, to):
        return pltpu.make_async_remote_copy(src, dst, send, recv, device_id=to, device_id_type=MESH)

    barrier = pltpu.get_barrier_semaphore()
    pl.semaphore_signal(barrier, 1, device_id=sibling, device_id_type=MESH)
    for k in range(1, nz):
        pl.semaphore_signal(barrier, 1, device_id=at_z(z + k), device_id_type=MESH)
    for k in range(1, ne):
        pl.semaphore_signal(barrier, 1, device_id={"exp": lax.rem(e + k, ne)}, device_id_type=MESH)

    pairs_in = (
        (ld_hbm, ld_ref), (x_hbm, x_ref), (b_hbm, b_ref), (c_hbm, c_ref), (skip_hbm, skip_ref), (r_hbm, r_ref), (rw_hbm, rw_ref),
        (gt_hbm, gt_ref),
    )
    loads = [pltpu.make_async_copy(src, dst, l_sem.at[k]) for k, (src, dst) in enumerate(pairs_in)]
    load_w = pltpu.make_async_copy(w_hbm, wbuf.at[z], l_sem.at[8])
    load_g = [pltpu.make_async_copy(g_hbm.at[:, k], gbuf.at[k], l_sem.at[9 + k]) for k in range(2)]
    load_w.start()
    for load in loads + load_g:
        load.start()
    load_w.wait()
    pl.semaphore_wait(barrier, 1 + nz - 1 + ne - 1)

    wrows = wbuf.shape[1] // WQ

    def w_hops(dd, q):
        return up if (q < WQ // 2) == (dd == 0) else up - 1

    def w_piece(chip, q):
        return wbuf.at[ring(chip), pl.ds(q * wrows, wrows), :]

    w_todo = [(i, q) for i in range(up + 1) for q in range(WQ)]

    def tick(n=1):
        for _ in range(n):
            i, q = w_todo.pop(0)
            for dd in range(2):
                turn, hops = 1 - 2 * dd, w_hops(dd, q)
                piece = w_piece(z - turn * i, q)
                if 0 < i <= hops:
                    await_bytes(piece, w_recv.at[dd, i - 1, q])
                if i < hops:
                    remote(piece, piece, w_send, w_recv.at[dd, i, q], at_z(z + turn)).start()

    tick(WQ)

    for load in loads[:3]:
        load.wait()

    ld = jnp.maximum(ld_ref[...], FLOOR)
    row, col = iota((tokens, tokens), 0), iota((tokens, tokens), 1)
    causal = row >= col
    cum = dot(causal.astype(f32), ld, ((1,), (1,)), HIGHEST)
    cum_t = dot(ld, (row <= col).astype(f32), precision=HIGHEST)
    spread = (iota((heads, width), 1) // hw == iota((heads, width), 0)).astype(f32)
    cum_x = dot(cum, spread, precision=HIGHEST)
    x = x_ref[...]
    xf = x.astype(f32)
    to_end = jnp.exp(cum_x[tokens - 1 :, :] - cum_x)
    span[...] = jnp.exp(cum_x[tokens - 1 :, :])
    lst[...] = dot(b_ref[...], (xf * to_end).astype(bf16), ((0,), (0,))).astype(bf16)
    own_state = remote(lst, lsib, l_send.at[0], l_recv.at[0], sibling)
    own_span = remote(span, span_sib, l_send.at[1], l_recv.at[1], sibling)
    own_state.start()
    own_span.start()

    for load in loads[3:]:
        load.wait()
    tick()
    scores = dot(c_ref[...], b_ref[...], ((1,), (1,)))

    def inner(h):
        gap = jnp.minimum(cum[:, h : h + 1] - cum_t[h : h + 1, :], 0.0)
        mixing = (jnp.where(causal, jnp.exp(gap), 0.0) * scores).astype(bf16)
        first_lane = h * hw // LANES * LANES
        return dot(mixing, x[:, first_lane : first_lane + LANES])

    inners = [inner(0)]
    tick()

    own_state.wait_recv()
    own_span.wait_recv()
    mine = pl.ds(pl.multiple_of(core * half, half), half)
    first, second = lst[:, mine].astype(f32), lsib[:, mine].astype(f32)
    decay_own, decay_sib = span[:, mine], span_sib[:, mine]
    is0 = core == 0
    joined = jnp.where(is0, decay_sib, decay_own) * jnp.where(is0, first, second) + jnp.where(is0, second, first)
    joined = joined.astype(bf16)
    lane_blocks = half // LANES
    for j in range(nz):
        rb, lb = j // lane_blocks, j % lane_blocks
        stb[j] = joined[rb * 16 : (rb + 1) * 16, lb * LANES : (lb + 1) * LANES]
    decay = decay_own * decay_sib
    tick()
    for lb in range(lane_blocks):
        dec[lb] = decay[:, lb * LANES : (lb + 1) * LANES]
    for k in range(1, nz):
        j = lax.rem(z + k, nz)
        remote(stb.at[j], rs.at[z], s1_send, s1_recv, at_z(j)).start()
        remote(dec.at[lax.rem(j, lane_blocks)], rd.at[z], d1_send, d1_recv, at_z(j)).start()
    rs[pl.ds(z, 1)] = stb[pl.ds(z, 1)]
    rd[pl.ds(z, 1)] = dec[pl.ds(lax.rem(z, lane_blocks), 1)]

    for h in range(1, 5):
        tick()
        inners.append(inner(h))
    tick()
    await_bytes(rs.at[pl.ds(0, nz - 1)], s1_recv)
    await_bytes(rd.at[pl.ds(0, nz - 1)], d1_recv)
    state = jnp.zeros(rs.shape[1:], f32)
    for j in range(nz):
        if j == nz // 2:
            tick()
        pre[j] = state.astype(bf16)
        state = rd[j] * state + rs[j].astype(f32)
    tick()
    place = (pl.ds(pl.multiple_of(z // lane_blocks * 16, 16), 16), pl.ds(pl.multiple_of(z % lane_blocks * LANES, LANES), LANES))
    for k in range(1, nz):
        j = lax.rem(z + k, nz)
        remote(pre.at[j], ent.at[core, place[0], place[1]], s2_send, s2_recv, at_z(j)).start()
    ent[core, place[0], place[1]] = pre[z]

    for h in range(5, heads):
        tick()
        inners.append(inner(h))
    per = LANES // hw
    pairs = []
    for p in range(width // LANES):
        part = inners[p * per]
        for k in range(1, per):
            part = jnp.where(iota(part.shape, 1) // hw == k, inners[p * per + k], part)
        pairs.append(part)
    tick()
    within = jnp.concatenate(pairs, axis=1) + dot(skip_ref[...], spread, precision=HIGHEST) * xf
    tick()

    before = ((row // SOURCE == col // SOURCE) & (row < col)).astype(bf16)

    def rows_of(ref, k):
        return jnp.concatenate([ref[k : k + 1, j * tokens : (j + 1) * tokens] for j in range(nc)], axis=0)

    own0, own1 = rows_of(r_ref, 0) == e, rows_of(r_ref, 1) == e
    own = own0 | own1
    tick()
    own_pos = dot(own.astype(bf16), before)
    first_slot = (iota((nc, tokens), 1) // SOURCE * CAP).astype(f32)
    goal_ref[...] = jnp.where(own, first_slot + own_pos, -1.0)
    value_ref[...] = jnp.where(own0, rows_of(rw_ref, 0), jnp.where(own1, rows_of(rw_ref, 1), 0.0))

    tick()

    await_bytes(pre.at[pl.ds(0, nz - 1)], s2_recv)
    entering = remote(ent.at[core], ent.at[core], e_send, e_recv, sibling)
    entering.start()
    tick(2)
    await_bytes(ent.at[1 - core], e_recv)
    carried = jnp.concatenate([ent[0], ent[1]], axis=1)
    after0 = (span_sib[...] * carried.astype(f32) + lsib[...].astype(f32)).astype(bf16)
    carried = jnp.where(is0, carried.astype(f32), after0.astype(f32)).astype(bf16)
    tick()
    overall = within + dot(c_ref[...], carried) * jnp.exp(cum_x)
    tick()
    gall[pl.ds(core, 1)] = (overall * silu(gt_ref[...].astype(f32))).astype(bf16)[None]
    both_cores = remote(gall.at[core], gall.at[core], g_send, g_recv, sibling)
    both_cores.start()

    def send_part(part, j):
        @pl.when(j != e)
        def _():
            remote(psend.at[part, j], precv.at[part, e], p_send.at[part], p_recv.at[part], {"exp": j}).start()

    def project(first_chip, count, at_once):
        chips = [ring(first_chip + lax.rem(e + k, count)) for k in range(count)]
        for k in range(0, count, 2):
            some = chips[k : k + 2]
            out = dot(gall[...].reshape(2 * tokens, width), jnp.concatenate([wbuf[j] for j in some], axis=1)).astype(bf16)
            for s, j in enumerate(some):
                for part in range(2):
                    psend[part, j] = out[part * tokens : (part + 1) * tokens, s * LANES : (s + 1) * LANES]
                send_part(0, j)
                if at_once:
                    send_part(1, j)
            tick(min(2, len(w_todo)))
        if not at_once:
            for j in chips:
                send_part(1, j)

    def summed(part):
        precv[part, pl.ds(e, 1)] = psend[part, pl.ds(e, 1)]
        await_bytes(psend.at[part, pl.ds(0, ne - 1)], p_recv.at[part])
        total = precv[part, 0].astype(f32)
        for k in range(1, ne):
            total += precv[part, k].astype(f32)
        return total.astype(bf16)

    tick(max(1, len(w_todo) - WQ * (up - NEAR)))
    await_bytes(gall.at[1 - core], g_recv)
    project(z - NEAR, 2 * NEAR + 1, True)
    tick(len(w_todo))
    project(z + NEAR + 1, nz - 2 * NEAR - 1, False)

    def to_slots(block, values):
        at = pl.ds(pl.multiple_of(block * tokens, tokens), tokens)
        experts = iota((ne, tokens), 0)
        hit = (r_ref[0:1, at] == experts) | (r_ref[1:2, at] == experts)
        pos = dot(hit.astype(bf16), before).astype(jnp.int32)
        target = jnp.where(hit, iota((ne, tokens), 1) // SOURCE * CAP + pos, -1)
        masks = (target[:, None, :] == iota((ne, slots, tokens), 1)).astype(f32).astype(bf16)
        return dot(masks.reshape(ne * slots, tokens), values).astype(bf16).reshape(ne, slots, values.shape[1])

    lane = pl.ds(pl.multiple_of(e * LANES, LANES), LANES)
    dsend[...] = to_slots(z * 2, summed(0))
    for k in range(1, ne):
        j = lax.rem(e + k, ne)
        remote(dsend.at[j], abuf.at[z, core, :, lane], m_send, m_recv, {"exp": j}).start()
    abuf[z, core, :, lane] = dsend[e]

    second_half = summed(1)
    mbuf[0, 0] = second_half
    mbuf[1, 0] = second_half

    def b_ring(i):
        for dd in range(2):
            turn, hops = 1 - 2 * dd, up - dd

            @pl.when((i > 0) & (i <= hops))
            def _():
                await_bytes(mbuf.at[dd, i], b_recv.at[dd, lax.rem(i + up - 1, up)])

            @pl.when(i < hops)
            def _():
                remote(mbuf.at[dd, i], mbuf.at[dd, i + 1], b_send.at[dd], b_recv.at[dd, lax.rem(i, up)], at_z(z + turn)).start()

    def b_dispatch(dd, i):
        chip = ring(z - (1 - 2 * dd) * i)
        bsend[chip] = to_slots(chip * 2 + 1, mbuf[dd, i])

        def one(k, _):
            j = lax.rem(e + k, ne)
            remote(bsend.at[chip, j], bbuf.at[chip, core, :, lane], bd_send, bd_recv.at[chip], {"exp": j}).start()
            return 0

        lax.fori_loop(1, ne, one, 0)
        bbuf[chip, core, :, lane] = bsend[chip, e]

    def b_side(dd, i):
        chip = ring(z - (1 - 2 * dd) * i)
        await_bytes(bsend.at[chip, pl.ds(0, ne - 1)], bd_recv.at[chip])
        block = bbuf.at[chip, core]
        remote(block, block, bs_send, bs_recv.at[chip], sibling).start()

    acols = abuf.shape[3] // AQ

    def a_ring(i, q):
        for dd in range(2):
            turn, hops = 1 - 2 * dd, up if (q < AQ // 2) == (dd == 0) else up - 1
            piece = abuf.at[ring(z - turn * i), core, :, pl.ds(q * acols, acols)]

            @pl.when((i > 0) & (i <= hops))
            def _():
                await_bytes(piece, a_recv.at[dd, lax.rem(i + up - 1, up), q])

            @pl.when(i < hops)
            def _():
                remote(piece, piece, a_send, a_recv.at[dd, lax.rem(i, up), q], at_z(z + turn)).start()

    def a_side(dd, i):
        chip = ring(z - (1 - 2 * dd) * i)
        block = abuf.at[chip, core]
        remote(block, block, as_send, as_recv.at[chip], sibling).start()

    def expert(i):
        chips = (ring(z - i), ring(z + lax.rem(i, up)))
        for chip in chips:
            await_bytes(abuf.at[chip, 1 - core], as_recv.at[chip])
            await_bytes(bbuf.at[chip, 1 - core], bs_recv.at[chip])

        product = None
        for p in range(2):
            rows = jnp.concatenate([buf[chip, p] for chip in chips for buf in (abuf, bbuf)], axis=0)
            part = dot(rows, gbuf[p].reshape(rows.shape[1], gbuf.shape[3]))
            product = part if product is None else product + part
        for k, chip in enumerate(chips):
            weights = []
            for s in range(2):
                goal, value = goal_ref[pl.ds(chip * 2 + s, 1), :], value_ref[pl.ds(chip * 2 + s, 1), :]
                at = goal == iota((slots, tokens), 0).astype(f32)
                weights.append(jnp.sum(jnp.where(at, value, 0.0), axis=1, keepdims=True))
            weight = jnp.concatenate(weights, axis=0)
            part = product[k * 2 * slots : (k + 1) * 2 * slots]
            out_ref[0, pl.ds(pl.multiple_of(chip * 2 * slots, 2 * slots), 2 * slots), :] = (weight * silu(part)).astype(bf16)

    def step(i, _):
        b_ring(i)
        a_ring(i - 1, 0)

        @pl.when(i <= up)
        def _():
            b_dispatch(0, i)

        a_ring(i - 1, 1)

        @pl.when(i < up)
        def _():
            b_dispatch(1, i)

        a_ring(i - 1, 2)

        @pl.when(i <= up + 1)
        def _():
            b_side(0, i - 1)

        @pl.when((i > 1) & (i < up + 1))
        def _():
            b_side(1, i - 1)

        a_ring(i - 1, 3)

        @pl.when(i <= up + 1)
        def _():
            a_side(0, i - 1)

        @pl.when((i > 1) & (i < up + 1))
        def _():
            a_side(1, i - 1)

        @pl.when(i > 2)
        def _():
            expert(i - 2)

        return 0

    b_ring(0)
    b_dispatch(0, 0)
    for load in load_g:
        load.wait()
    await_bytes(dsend.at[pl.ds(0, ne - 1)], m_recv)
    lax.fori_loop(1, up + 3, step, 0)

    own_state.wait_send()
    own_span.wait_send()
    entering.wait_send()
    await_bytes(stb.at[pl.ds(0, nz - 1)], s1_send)
    await_bytes(rd.at[pl.ds(0, nz - 1)], d1_send)
    await_bytes(pre.at[pl.ds(0, nz - 1)], s2_send)
    await_bytes(wbuf.at[pl.ds(0, nz - 1)], w_send)
    both_cores.wait_send()
    for part in range(2):
        await_bytes(psend.at[part, pl.ds(0, ne - 1)], p_send.at[part])
    await_bytes(dsend.at[pl.ds(0, ne - 1)], m_send)
    await_bytes(abuf.at[pl.ds(0, nz - 1), 0], a_send)
    await_bytes(abuf.at[:, 0], as_send)
    for dd in range(2):
        await_bytes(mbuf.at[dd, pl.ds(0, up - dd)], b_send.at[dd])
    await_bytes(bsend.at[:, pl.ds(0, ne - 1)], bd_send)
    await_bytes(bbuf.at[:, 0], bs_send)


def body(x, gt, b, c, ld, skip, w, routes, weights, gate):
    nc, ne = lax.axis_size("ctx"), lax.axis_size("exp")
    nz = nc // 2
    tokens, width = x.shape
    heads = ld.shape[1]
    depth, shard = w.shape
    wide = shard * nc
    slots = tokens // SOURCE * CAP
    ff = gate.shape[2]
    blocks = width // 2 // LANES
    hbm = pl.BlockSpec(memory_space=pl.ANY)
    dma = pltpu.SemaphoreType.DMA
    r = routes.T
    rw = weights.T.astype(f32)

    def vmem(shape, kind=bf16):
        return pltpu.VMEM(shape, kind)

    return pl.pallas_call(
        kernel,
        out_shape=jax.ShapeDtypeStruct((1, nc * slots, ff), bf16),
        in_specs=[hbm] * 10,
        out_specs=pl.BlockSpec(memory_space=pltpu.VMEM),
        scratch_shapes=[
            vmem(x.shape), vmem(gt.shape), vmem(b.shape), vmem(c.shape), vmem((heads, tokens), f32), vmem((1, heads), f32),
            vmem(r.shape, jnp.int32), vmem(rw.shape, f32),
            vmem((2, ne, LANES, ff)), vmem((nz, depth, shard)),
            vmem((nz, 2, slots, wide // 2)), vmem((nz, 2, slots, wide // 2)),
            vmem((2, ne, tokens, LANES)), vmem((2, ne, tokens, LANES)),
            vmem((ne, slots, LANES)), vmem((nz, ne, slots, LANES)), vmem((2, nz // 2 + 1, tokens, LANES)),
            vmem((2, *x.shape)), vmem((b.shape[1], width)), vmem((b.shape[1], width)), vmem((1, width), f32), vmem((1, width), f32),
            vmem((nz, 16, LANES)), vmem((blocks, 1, LANES), f32), vmem((nz, 16, LANES)), vmem((nz, 1, LANES), f32),
            vmem((nz, 16, LANES)), vmem((2, b.shape[1], width // 2)),
            vmem((nc, tokens), f32), vmem((nc, tokens), f32),
            dma((11,)), dma((2,)), dma((2,)), dma, dma, dma, dma, dma, dma, dma, dma,
            dma, dma((2, nz // 2, WQ)), dma, dma,
            dma((2,)), dma((2,)), dma, dma,
            dma, dma((2, nz // 2, AQ)), dma, dma((nz,)),
            dma((2,)), dma((2, nz // 2)), dma, dma((nz,)), dma, dma((nz,)),
        ],
        compiler_params=pltpu.CompilerParams(
            collective_id=0, has_side_effects=True, vmem_limit_bytes=56 * 2**20
        ),
        name="hybrid_block",
    )(x, gt, b, c, ld.T, skip.reshape(1, heads), w, r, rw, gate.reshape(ne, 2, LANES, ff))


def solution(mesh):
    in_specs = (
        P("ctx", "exp"),
        P("ctx", "exp"),
        P("ctx", None),
        P("ctx", None),
        P("ctx", "exp"),
        P("exp"),
        P("exp", "ctx"),
        P(),
        P(),
        P("exp", None, "ctx"),
    )
    out_specs = P("exp", None, "ctx")
    return jax.shard_map(body, mesh=mesh, in_specs=in_specs, out_specs=out_specs, check_vma=False)
```

```python
import jax
import jax.numpy as jnp
from jax import lax
from jax.experimental import pallas as pl
from jax.experimental.pallas import tpu as pltpu
from jax.sharding import PartitionSpec as P

MESH = pl.DeviceIdType.MESH
SOURCE = 8
CAP = 2
FLOOR = -110.0
HIGHEST = lax.Precision.HIGHEST
WQ = 4
AQ = 4
NEAR, MIDDLE = 3, 5
LANES = 128
bf16 = jnp.bfloat16
f32 = jnp.float32


def dot(a, b, dims=((1,), (0,)), precision=None):
    return lax.dot_general(a, b, (dims, ((), ())), preferred_element_type=f32, precision=precision)


def iota(shape, dim):
    return lax.broadcasted_iota(jnp.int32, shape, dim)


def silu(v):
    return v / (1.0 + jnp.exp(-v))


def await_bytes(ref, sem):
    pltpu.make_async_copy(ref, ref, sem).wait()


def kernel(
    x_hbm, gt_hbm, b_hbm, c_hbm, ld_hbm, skip_hbm, w_hbm, r_hbm, rw_hbm, g_hbm,
    out_ref,
    x_ref, gt_ref, b_ref, c_ref, ld_ref, skip_ref, r_ref, rw_ref, gbuf, wbuf, abuf, bbuf, psend, precv, dsend, bsend, mbuf,
    gall, lst, lsib, span, span_sib, stb, dec, rs, rd, pre, ent, goal_ref, value_ref,
    l_sem, l_send, l_recv, s1_send, s1_recv, d1_send, d1_recv, s2_send, s2_recv, e_send, e_recv,
    w_send, w_recv, g_send, g_recv, p_send, p_recv, m_send, m_recv, a_send, a_recv, as_send, as_recv,
    b_send, b_recv, bd_send, bd_recv, bs_send, bs_recv,
):
    nc, ne = lax.axis_size("ctx"), lax.axis_size("exp")
    nz = nc // 2
    up = nz // 2
    c, e = lax.axis_index("ctx"), lax.axis_index("exp")
    z, core = c // 2, c % 2
    tokens, width = x_ref.shape
    heads = ld_ref.shape[0]
    hw = width // heads
    half = width // 2
    slots = tokens // SOURCE * CAP
    sibling = {"ctx": c + 1 - 2 * core}

    def ring(chip):
        return lax.rem(chip + nz, nz)

    def at_z(chip):
        return {"ctx": ring(chip) * 2 + core}

    def remote(src, dst, send, recv, to):
        return pltpu.make_async_remote_copy(src, dst, send, recv, device_id=to, device_id_type=MESH)

    barrier = pltpu.get_barrier_semaphore()
    pl.semaphore_signal(barrier, 1, device_id=sibling, device_id_type=MESH)
    for k in range(1, nz):
        pl.semaphore_signal(barrier, 1, device_id=at_z(z + k), device_id_type=MESH)
    for k in range(1, ne):
        pl.semaphore_signal(barrier, 1, device_id={"exp": lax.rem(e + k, ne)}, device_id_type=MESH)

    pairs_in = (
        (ld_hbm, ld_ref), (x_hbm, x_ref), (b_hbm, b_ref), (c_hbm, c_ref), (skip_hbm, skip_ref), (r_hbm, r_ref), (rw_hbm, rw_ref),
        (gt_hbm, gt_ref),
    )
    loads = [pltpu.make_async_copy(src, dst, l_sem.at[k]) for k, (src, dst) in enumerate(pairs_in)]
    load_w = pltpu.make_async_copy(w_hbm, wbuf.at[z], l_sem.at[8])
    load_g = [pltpu.make_async_copy(g_hbm.at[:, k], gbuf.at[k], l_sem.at[9 + k]) for k in range(2)]
    load_w.start()
    for load in loads + load_g:
        load.start()
    load_w.wait()
    pl.semaphore_wait(barrier, 1 + nz - 1 + ne - 1)

    wrows = wbuf.shape[1] // WQ

    def w_hops(dd, q):
        return up if (q < WQ // 2) == (dd == 0) else up - 1

    def w_piece(chip, q):
        return wbuf.at[ring(chip), pl.ds(q * wrows, wrows), :]

    w_todo = [(i, q) for i in range(up + 1) for q in range(WQ)]

    def tick(n=1):
        for _ in range(min(n, len(w_todo))):
            i, q = w_todo.pop(0)
            for dd in range(2):
                turn, hops = 1 - 2 * dd, w_hops(dd, q)
                piece = w_piece(z - turn * i, q)
                if 0 < i <= hops:
                    await_bytes(piece, w_recv.at[dd, i - 1, q])
                if i < hops:
                    remote(piece, piece, w_send, w_recv.at[dd, i, q], at_z(z + turn)).start()

    tick(WQ)

    for load in loads[:3]:
        load.wait()

    ld = jnp.maximum(ld_ref[...], FLOOR)
    row, col = iota((tokens, tokens), 0), iota((tokens, tokens), 1)
    causal = row >= col
    cum = dot(causal.astype(f32), ld, ((1,), (1,)), HIGHEST)
    cum_t = dot(ld, (row <= col).astype(f32), precision=HIGHEST)
    spread = (iota((heads, width), 1) // hw == iota((heads, width), 0)).astype(f32)
    cum_x = dot(cum, spread, precision=HIGHEST)
    x = x_ref[...]
    xf = x.astype(f32)
    to_end = jnp.exp(cum_x[tokens - 1 :, :] - cum_x)
    span[...] = jnp.exp(cum_x[tokens - 1 :, :])
    lst[...] = dot(b_ref[...], (xf * to_end).astype(bf16), ((0,), (0,))).astype(bf16)
    own_state = remote(lst, lsib, l_send.at[0], l_recv.at[0], sibling)
    own_span = remote(span, span_sib, l_send.at[1], l_recv.at[1], sibling)
    own_state.start()
    own_span.start()

    for load in loads[3:]:
        load.wait()
    tick()
    scores = dot(c_ref[...], b_ref[...], ((1,), (1,)))

    def inner(h):
        gap = jnp.minimum(cum[:, h : h + 1] - cum_t[h : h + 1, :], 0.0)
        mixing = (jnp.where(causal, jnp.exp(gap), 0.0) * scores).astype(bf16)
        first_lane = h * hw // LANES * LANES
        return dot(mixing, x[:, first_lane : first_lane + LANES])

    inners = [inner(0)]
    tick()

    own_state.wait_recv()
    own_span.wait_recv()
    mine = pl.ds(pl.multiple_of(core * half, half), half)
    first, second = lst[:, mine].astype(f32), lsib[:, mine].astype(f32)
    decay_own, decay_sib = span[:, mine], span_sib[:, mine]
    is0 = core == 0
    joined = jnp.where(is0, decay_sib, decay_own) * jnp.where(is0, first, second) + jnp.where(is0, second, first)
    joined = joined.astype(bf16)
    lane_blocks = half // LANES
    for j in range(nz):
        rb, lb = j // lane_blocks, j % lane_blocks
        stb[j] = joined[rb * 16 : (rb + 1) * 16, lb * LANES : (lb + 1) * LANES]
    decay = decay_own * decay_sib
    tick()
    for lb in range(lane_blocks):
        dec[lb] = decay[:, lb * LANES : (lb + 1) * LANES]
    for k in range(1, nz):
        j = lax.rem(z + k, nz)
        remote(stb.at[j], rs.at[z], s1_send, s1_recv, at_z(j)).start()
        remote(dec.at[lax.rem(j, lane_blocks)], rd.at[z], d1_send, d1_recv, at_z(j)).start()
    rs[pl.ds(z, 1)] = stb[pl.ds(z, 1)]
    rd[pl.ds(z, 1)] = dec[pl.ds(lax.rem(z, lane_blocks), 1)]

    for h in range(1, 5):
        tick()
        inners.append(inner(h))
    tick()
    await_bytes(rs.at[pl.ds(0, nz - 1)], s1_recv)
    await_bytes(rd.at[pl.ds(0, nz - 1)], d1_recv)
    state = jnp.zeros(rs.shape[1:], f32)
    for j in range(nz):
        if j == nz // 2:
            tick()
        pre[j] = state.astype(bf16)
        state = rd[j] * state + rs[j].astype(f32)
    tick()
    place = (pl.ds(pl.multiple_of(z // lane_blocks * 16, 16), 16), pl.ds(pl.multiple_of(z % lane_blocks * LANES, LANES), LANES))
    for k in range(1, nz):
        j = lax.rem(z + k, nz)
        remote(pre.at[j], ent.at[core, place[0], place[1]], s2_send, s2_recv, at_z(j)).start()
    ent[core, place[0], place[1]] = pre[z]

    for h in range(5, heads):
        tick()
        inners.append(inner(h))
    per = LANES // hw
    pairs = []
    for p in range(width // LANES):
        part = inners[p * per]
        for k in range(1, per):
            part = jnp.where(iota(part.shape, 1) // hw == k, inners[p * per + k], part)
        pairs.append(part)
    tick()
    within = jnp.concatenate(pairs, axis=1) + dot(skip_ref[...], spread, precision=HIGHEST) * xf
    tick()

    before = ((row // SOURCE == col // SOURCE) & (row < col)).astype(bf16)

    def rows_of(ref, k):
        return jnp.concatenate([ref[k : k + 1, j * tokens : (j + 1) * tokens] for j in range(nc)], axis=0)

    own0, own1 = rows_of(r_ref, 0) == e, rows_of(r_ref, 1) == e
    own = own0 | own1
    tick()
    own_pos = dot(own.astype(bf16), before)
    first_slot = (iota((nc, tokens), 1) // SOURCE * CAP).astype(f32)
    goal_ref[...] = jnp.where(own, first_slot + own_pos, -1.0)
    value_ref[...] = jnp.where(own0, rows_of(rw_ref, 0), jnp.where(own1, rows_of(rw_ref, 1), 0.0))

    tick()

    await_bytes(pre.at[pl.ds(0, nz - 1)], s2_recv)
    entering = remote(ent.at[core], ent.at[core], e_send, e_recv, sibling)
    entering.start()
    tick(2)
    await_bytes(ent.at[1 - core], e_recv)
    carried = jnp.concatenate([ent[0], ent[1]], axis=1)
    after0 = (span_sib[...] * carried.astype(f32) + lsib[...].astype(f32)).astype(bf16)
    carried = jnp.where(is0, carried.astype(f32), after0.astype(f32)).astype(bf16)
    tick()
    overall = within + dot(c_ref[...], carried) * jnp.exp(cum_x)
    tick()
    gall[pl.ds(core, 1)] = (overall * silu(gt_ref[...].astype(f32))).astype(bf16)[None]
    both_cores = remote(gall.at[core], gall.at[core], g_send, g_recv, sibling)
    both_cores.start()

    def send_part(part, j):
        @pl.when(j != e)
        def _():
            remote(psend.at[part, j], precv.at[part, e], p_send.at[part], p_recv.at[part], {"exp": j}).start()

    def project(chips, ticks, at_once):
        for k in range(0, len(chips), 2):
            some = chips[k : k + 2]
            out = dot(gall[...].reshape(2 * tokens, width), jnp.concatenate([wbuf[j] for j in some], axis=1)).astype(bf16)
            for s, j in enumerate(some):
                for part in range(2):
                    psend[part, j] = out[part * tokens : (part + 1) * tokens, s * LANES : (s + 1) * LANES]
                send_part(0, j)
                if at_once:
                    send_part(1, j)
            tick(ticks)
        if not at_once:
            for j in chips:
                send_part(1, j)

    def within_reach(apart):
        tick(max(0, len(w_todo) - WQ * (up - apart)))

    def summed(part):
        precv[part, pl.ds(e, 1)] = psend[part, pl.ds(e, 1)]
        await_bytes(psend.at[part, pl.ds(0, ne - 1)], p_recv.at[part])
        total = precv[part, 0].astype(f32)
        for k in range(1, ne):
            total += precv[part, k].astype(f32)
        return total.astype(bf16)

    await_bytes(gall.at[1 - core], g_recv)
    count = 2 * NEAR + 1
    within_reach(NEAR)
    project([ring(z - NEAR + lax.rem(e + k, count)) for k in range(count)], 2, True)
    count = 2 * (MIDDLE - NEAR)
    within_reach(MIDDLE)
    turns = [lax.rem(e + k, count) for k in range(count)]
    project([ring(z + (1 - 2 * (t % 2)) * (NEAR + 1 + t // 2)) for t in turns], 2, True)
    count = nz - 2 * MIDDLE - 1
    within_reach(up)
    project([ring(z + MIDDLE + 1 + lax.rem(e + k, count)) for k in range(count)], 0, False)

    def to_slots(block, values):
        at = pl.ds(pl.multiple_of(block * tokens, tokens), tokens)
        experts = iota((ne, tokens), 0)
        hit = (r_ref[0:1, at] == experts) | (r_ref[1:2, at] == experts)
        pos = dot(hit.astype(bf16), before).astype(jnp.int32)
        target = jnp.where(hit, iota((ne, tokens), 1) // SOURCE * CAP + pos, -1)
        masks = (target[:, None, :] == iota((ne, slots, tokens), 1)).astype(f32).astype(bf16)
        return dot(masks.reshape(ne * slots, tokens), values).astype(bf16).reshape(ne, slots, values.shape[1])

    lane = pl.ds(pl.multiple_of(e * LANES, LANES), LANES)
    dsend[...] = to_slots(z * 2, summed(0))
    for k in range(1, ne):
        j = lax.rem(e + k, ne)
        remote(dsend.at[j], abuf.at[z, core, :, lane], m_send, m_recv, {"exp": j}).start()
    abuf[z, core, :, lane] = dsend[e]

    second_half = summed(1)
    mbuf[0, 0] = second_half
    mbuf[1, 0] = second_half

    def b_ring(i):
        for dd in range(2):
            turn, hops = 1 - 2 * dd, up - dd

            @pl.when((i > 0) & (i <= hops))
            def _():
                await_bytes(mbuf.at[dd, i], b_recv.at[dd, lax.rem(i + up - 1, up)])

            @pl.when(i < hops)
            def _():
                remote(mbuf.at[dd, i], mbuf.at[dd, i + 1], b_send.at[dd], b_recv.at[dd, lax.rem(i, up)], at_z(z + turn)).start()

    def b_dispatch(dd, i):
        chip = ring(z - (1 - 2 * dd) * i)
        bsend[chip] = to_slots(chip * 2 + 1, mbuf[dd, i])

        def one(k, _):
            j = lax.rem(e + k, ne)
            remote(bsend.at[chip, j], bbuf.at[chip, core, :, lane], bd_send, bd_recv.at[chip], {"exp": j}).start()
            return 0

        lax.fori_loop(1, ne, one, 0)
        bbuf[chip, core, :, lane] = bsend[chip, e]

    def b_side(dd, i):
        chip = ring(z - (1 - 2 * dd) * i)
        await_bytes(bsend.at[chip, pl.ds(0, ne - 1)], bd_recv.at[chip])
        block = bbuf.at[chip, core]
        remote(block, block, bs_send, bs_recv.at[chip], sibling).start()

    acols = abuf.shape[3] // AQ

    def a_ring(i, q):
        for dd in range(2):
            turn, hops = 1 - 2 * dd, up if (q < AQ // 2) == (dd == 0) else up - 1
            piece = abuf.at[ring(z - turn * i), core, :, pl.ds(q * acols, acols)]

            @pl.when((i > 0) & (i <= hops))
            def _():
                await_bytes(piece, a_recv.at[dd, lax.rem(i + up - 1, up), q])

            @pl.when(i < hops)
            def _():
                remote(piece, piece, a_send, a_recv.at[dd, lax.rem(i, up), q], at_z(z + turn)).start()

    def a_side(dd, i):
        chip = ring(z - (1 - 2 * dd) * i)
        block = abuf.at[chip, core]
        remote(block, block, as_send, as_recv.at[chip], sibling).start()

    def expert(i):
        chips = (ring(z - i), ring(z + lax.rem(i, up)))
        for chip in chips:
            await_bytes(abuf.at[chip, 1 - core], as_recv.at[chip])
            await_bytes(bbuf.at[chip, 1 - core], bs_recv.at[chip])

        product = None
        for p in range(2):
            rows = jnp.concatenate([buf[chip, p] for chip in chips for buf in (abuf, bbuf)], axis=0)
            part = dot(rows, gbuf[p].reshape(rows.shape[1], gbuf.shape[3]))
            product = part if product is None else product + part
        for k, chip in enumerate(chips):
            weights = []
            for s in range(2):
                goal, value = goal_ref[pl.ds(chip * 2 + s, 1), :], value_ref[pl.ds(chip * 2 + s, 1), :]
                at = goal == iota((slots, tokens), 0).astype(f32)
                weights.append(jnp.sum(jnp.where(at, value, 0.0), axis=1, keepdims=True))
            weight = jnp.concatenate(weights, axis=0)
            part = product[k * 2 * slots : (k + 1) * 2 * slots]
            out_ref[0, pl.ds(pl.multiple_of(chip * 2 * slots, 2 * slots), 2 * slots), :] = (weight * silu(part)).astype(bf16)

    def step(i, _):
        b_ring(i)
        a_ring(i - 1, 0)

        @pl.when(i <= up)
        def _():
            b_dispatch(0, i)

        a_ring(i - 1, 1)

        @pl.when(i < up)
        def _():
            b_dispatch(1, i)

        a_ring(i - 1, 2)

        @pl.when((i > 1) & (i <= up + 2))
        def _():
            b_side(0, i - 2)

        @pl.when((i > 2) & (i < up + 2))
        def _():
            b_side(1, i - 2)

        a_ring(i - 1, 3)

        @pl.when(i <= up + 1)
        def _():
            a_side(0, i - 1)

        @pl.when((i > 1) & (i < up + 1))
        def _():
            a_side(1, i - 1)

        @pl.when(i > 3)
        def _():
            expert(i - 3)

        return 0

    b_ring(0)
    b_dispatch(0, 0)
    for load in load_g:
        load.wait()
    await_bytes(dsend.at[pl.ds(0, ne - 1)], m_recv)
    lax.fori_loop(1, up + 4, step, 0)

    own_state.wait_send()
    own_span.wait_send()
    entering.wait_send()
    await_bytes(stb.at[pl.ds(0, nz - 1)], s1_send)
    await_bytes(rd.at[pl.ds(0, nz - 1)], d1_send)
    await_bytes(pre.at[pl.ds(0, nz - 1)], s2_send)
    await_bytes(wbuf.at[pl.ds(0, nz - 1)], w_send)
    both_cores.wait_send()
    for part in range(2):
        await_bytes(psend.at[part, pl.ds(0, ne - 1)], p_send.at[part])
    await_bytes(dsend.at[pl.ds(0, ne - 1)], m_send)
    await_bytes(abuf.at[pl.ds(0, nz - 1), 0], a_send)
    await_bytes(abuf.at[:, 0], as_send)
    for dd in range(2):
        await_bytes(mbuf.at[dd, pl.ds(0, up - dd)], b_send.at[dd])
    await_bytes(bsend.at[:, pl.ds(0, ne - 1)], bd_send)
    await_bytes(bbuf.at[:, 0], bs_send)


def body(x, gt, b, c, ld, skip, w, routes, weights, gate):
    nc, ne = lax.axis_size("ctx"), lax.axis_size("exp")
    nz = nc // 2
    tokens, width = x.shape
    heads = ld.shape[1]
    depth, shard = w.shape
    wide = shard * nc
    slots = tokens // SOURCE * CAP
    ff = gate.shape[2]
    blocks = width // 2 // LANES
    hbm = pl.BlockSpec(memory_space=pl.ANY)
    dma = pltpu.SemaphoreType.DMA
    r = routes.T
    rw = weights.T.astype(f32)

    def vmem(shape, kind=bf16):
        return pltpu.VMEM(shape, kind)

    return pl.pallas_call(
        kernel,
        out_shape=jax.ShapeDtypeStruct((1, nc * slots, ff), bf16),
        in_specs=[hbm] * 10,
        out_specs=pl.BlockSpec(memory_space=pltpu.VMEM),
        scratch_shapes=[
            vmem(x.shape), vmem(gt.shape), vmem(b.shape), vmem(c.shape), vmem((heads, tokens), f32), vmem((1, heads), f32),
            vmem(r.shape, jnp.int32), vmem(rw.shape, f32),
            vmem((2, ne, LANES, ff)), vmem((nz, depth, shard)),
            vmem((nz, 2, slots, wide // 2)), vmem((nz, 2, slots, wide // 2)),
            vmem((2, ne, tokens, LANES)), vmem((2, ne, tokens, LANES)),
            vmem((ne, slots, LANES)), vmem((nz, ne, slots, LANES)), vmem((2, nz // 2 + 1, tokens, LANES)),
            vmem((2, *x.shape)), vmem((b.shape[1], width)), vmem((b.shape[1], width)), vmem((1, width), f32), vmem((1, width), f32),
            vmem((nz, 16, LANES)), vmem((blocks, 1, LANES), f32), vmem((nz, 16, LANES)), vmem((nz, 1, LANES), f32),
            vmem((nz, 16, LANES)), vmem((2, b.shape[1], width // 2)),
            vmem((nc, tokens), f32), vmem((nc, tokens), f32),
            dma((11,)), dma((2,)), dma((2,)), dma, dma, dma, dma, dma, dma, dma, dma,
            dma, dma((2, nz // 2, WQ)), dma, dma,
            dma((2,)), dma((2,)), dma, dma,
            dma, dma((2, nz // 2, AQ)), dma, dma((nz,)),
            dma((2,)), dma((2, nz // 2)), dma, dma((nz,)), dma, dma((nz,)),
        ],
        compiler_params=pltpu.CompilerParams(
            collective_id=0, has_side_effects=True, vmem_limit_bytes=56 * 2**20
        ),
        name="hybrid_block",
    )(x, gt, b, c, ld.T, skip.reshape(1, heads), w, r, rw, gate.reshape(ne, 2, LANES, ff))


def solution(mesh):
    in_specs = (
        P("ctx", "exp"),
        P("ctx", "exp"),
        P("ctx", None),
        P("ctx", None),
        P("ctx", "exp"),
        P("exp"),
        P("exp", "ctx"),
        P(),
        P(),
        P("exp", None, "ctx"),
    )
    out_specs = P("exp", None, "ctx")
    return jax.shard_map(body, mesh=mesh, in_specs=in_specs, out_specs=out_specs, check_vma=False)
```

```python
import jax
import jax.numpy as jnp
from jax import lax
from jax.experimental import pallas as pl
from jax.experimental.pallas import tpu as pltpu
from jax.sharding import PartitionSpec as P

MESH = pl.DeviceIdType.MESH
SOURCE = 8
CAP = 2
FLOOR = -110.0
HIGHEST = lax.Precision.HIGHEST
WQ = 4
AQ = 4
NEAR, MIDDLE = 3, 5
LANES = 128
bf16 = jnp.bfloat16
f32 = jnp.float32


def dot(a, b, dims=((1,), (0,)), precision=None):
    return lax.dot_general(a, b, (dims, ((), ())), preferred_element_type=f32, precision=precision)


def iota(shape, dim):
    return lax.broadcasted_iota(jnp.int32, shape, dim)


def silu(v):
    return v / (1.0 + jnp.exp(-v))


def await_bytes(ref, sem):
    pltpu.make_async_copy(ref, ref, sem).wait()


def kernel(
    x_hbm, gt_hbm, b_hbm, c_hbm, ld_hbm, skip_hbm, w_hbm, r_hbm, rw_in, g_hbm,
    out_ref,
    x_ref, gt_ref, b_ref, c_ref, ld_ref, skip_ref, r_ref, rw_ref, gbuf, wbuf, abuf, bbuf, psend, precv, dsend, bsend, mbuf,
    gall, lst, lsib, span, span_sib, stb, dec, rs, rd, pre, ent, goal_ref, value_ref,
    l_sem, l_send, l_recv, s1_send, s1_recv, d1_send, d1_recv, s2_send, s2_recv, e_send, e_recv,
    w_send, w_recv, g_send, g_recv, p_send, p_recv, m_send, m_recv, a_send, a_recv, as_send, as_recv,
    b_send, b_recv, bd_send, bd_recv, bs_send, bs_recv,
):
    nc, ne = lax.axis_size("ctx"), lax.axis_size("exp")
    nz = nc // 2
    up = nz // 2
    c, e = lax.axis_index("ctx"), lax.axis_index("exp")
    z, core = c // 2, c % 2
    tokens, width = x_ref.shape
    heads = ld_ref.shape[0]
    hw = width // heads
    half = width // 2
    slots = tokens // SOURCE * CAP
    sibling = {"ctx": c + 1 - 2 * core}

    def ring(chip):
        return lax.rem(chip + nz, nz)

    def at_z(chip):
        return {"ctx": ring(chip) * 2 + core}

    def remote(src, dst, send, recv, to):
        return pltpu.make_async_remote_copy(src, dst, send, recv, device_id=to, device_id_type=MESH)

    barrier = pltpu.get_barrier_semaphore()
    pl.semaphore_signal(barrier, 1, device_id=sibling, device_id_type=MESH)
    for k in range(1, nz):
        pl.semaphore_signal(barrier, 1, device_id=at_z(z + k), device_id_type=MESH)
    for k in range(1, ne):
        pl.semaphore_signal(barrier, 1, device_id={"exp": lax.rem(e + k, ne)}, device_id_type=MESH)

    pairs_in = (
        (ld_hbm, ld_ref), (x_hbm, x_ref), (b_hbm, b_ref), (c_hbm, c_ref), (skip_hbm, skip_ref), (r_hbm, r_ref),
        (gt_hbm, gt_ref),
    )
    loads = [pltpu.make_async_copy(src, dst, l_sem.at[k]) for k, (src, dst) in enumerate(pairs_in)]
    load_w = pltpu.make_async_copy(w_hbm, wbuf.at[z], l_sem.at[7])
    load_g = [pltpu.make_async_copy(g_hbm.at[:, k], gbuf.at[k], l_sem.at[8 + k]) for k in range(2)]
    load_w.start()
    for load in loads + load_g:
        load.start()
    load_w.wait()
    pl.semaphore_wait(barrier, 1 + nz - 1 + ne - 1)

    wrows = wbuf.shape[1] // WQ

    def w_hops(dd, q):
        return up if (q < WQ // 2) == (dd == 0) else up - 1

    def w_piece(chip, q):
        return wbuf.at[ring(chip), pl.ds(q * wrows, wrows), :]

    w_todo = [(i, q) for i in range(up + 1) for q in range(WQ)]

    def tick(n=1):
        for _ in range(min(n, len(w_todo))):
            i, q = w_todo.pop(0)
            for dd in range(2):
                turn, hops = 1 - 2 * dd, w_hops(dd, q)
                piece = w_piece(z - turn * i, q)
                if 0 < i <= hops:
                    await_bytes(piece, w_recv.at[dd, i - 1, q])
                if i < hops:
                    remote(piece, piece, w_send, w_recv.at[dd, i, q], at_z(z + turn)).start()

    tick(WQ)

    for load in loads[:3]:
        load.wait()

    ld = jnp.maximum(ld_ref[...], FLOOR)
    row, col = iota((tokens, tokens), 0), iota((tokens, tokens), 1)
    causal = row >= col
    cum = dot(causal.astype(f32), ld, ((1,), (1,)), HIGHEST)
    cum_t = dot(ld, (row <= col).astype(f32), precision=HIGHEST)
    spread = (iota((heads, width), 1) // hw == iota((heads, width), 0)).astype(f32)
    cum_x = dot(cum, spread, precision=HIGHEST)
    x = x_ref[...]
    xf = x.astype(f32)
    to_end = jnp.exp(cum_x[tokens - 1 :, :] - cum_x)
    span[...] = jnp.exp(cum_x[tokens - 1 :, :])
    lst[...] = dot(b_ref[...], (xf * to_end).astype(bf16), ((0,), (0,))).astype(bf16)
    own_state = remote(lst, lsib, l_send.at[0], l_recv.at[0], sibling)
    own_span = remote(span, span_sib, l_send.at[1], l_recv.at[1], sibling)
    own_state.start()
    own_span.start()

    for load in loads[3:]:
        load.wait()
    tick()
    scores = dot(c_ref[...], b_ref[...], ((1,), (1,)))

    def inner(h):
        gap = jnp.minimum(cum[:, h : h + 1] - cum_t[h : h + 1, :], 0.0)
        mixing = (jnp.where(causal, jnp.exp(gap), 0.0) * scores).astype(bf16)
        first_lane = h * hw // LANES * LANES
        return dot(mixing, x[:, first_lane : first_lane + LANES])

    inners = [inner(0)]
    tick()

    own_state.wait_recv()
    own_span.wait_recv()
    mine = pl.ds(pl.multiple_of(core * half, half), half)
    first, second = lst[:, mine].astype(f32), lsib[:, mine].astype(f32)
    decay_own, decay_sib = span[:, mine], span_sib[:, mine]
    is0 = core == 0
    joined = jnp.where(is0, decay_sib, decay_own) * jnp.where(is0, first, second) + jnp.where(is0, second, first)
    joined = joined.astype(bf16)
    lane_blocks = half // LANES
    for j in range(nz):
        rb, lb = j // lane_blocks, j % lane_blocks
        stb[j] = joined[rb * 16 : (rb + 1) * 16, lb * LANES : (lb + 1) * LANES]
    decay = decay_own * decay_sib
    tick()
    for lb in range(lane_blocks):
        dec[lb] = decay[:, lb * LANES : (lb + 1) * LANES]
    for k in range(1, nz):
        j = lax.rem(z + k, nz)
        remote(stb.at[j], rs.at[z], s1_send, s1_recv, at_z(j)).start()
        remote(dec.at[lax.rem(j, lane_blocks)], rd.at[z], d1_send, d1_recv, at_z(j)).start()
    rs[pl.ds(z, 1)] = stb[pl.ds(z, 1)]
    rd[pl.ds(z, 1)] = dec[pl.ds(lax.rem(z, lane_blocks), 1)]

    for h in range(1, 5):
        tick()
        inners.append(inner(h))
    tick()
    await_bytes(rs.at[pl.ds(0, nz - 1)], s1_recv)
    await_bytes(rd.at[pl.ds(0, nz - 1)], d1_recv)
    state = jnp.zeros(rs.shape[1:], f32)
    for j in range(nz):
        if j == nz // 2:
            tick()
        pre[j] = state.astype(bf16)
        state = rd[j] * state + rs[j].astype(f32)
    tick()
    place = (pl.ds(pl.multiple_of(z // lane_blocks * 16, 16), 16), pl.ds(pl.multiple_of(z % lane_blocks * LANES, LANES), LANES))
    for k in range(1, nz):
        j = lax.rem(z + k, nz)
        remote(pre.at[j], ent.at[core, place[0], place[1]], s2_send, s2_recv, at_z(j)).start()
    ent[core, place[0], place[1]] = pre[z]

    for h in range(5, heads):
        tick()
        inners.append(inner(h))
    per = LANES // hw
    pairs = []
    for p in range(width // LANES):
        part = inners[p * per]
        for k in range(1, per):
            part = jnp.where(iota(part.shape, 1) // hw == k, inners[p * per + k], part)
        pairs.append(part)
    tick()
    within = jnp.concatenate(pairs, axis=1) + dot(skip_ref[...], spread, precision=HIGHEST) * xf
    tick()

    before = ((row // SOURCE == col // SOURCE) & (row < col)).astype(bf16)

    rw_ref[...] = rw_in[...].astype(f32)

    def rows_of(ref, k):
        return jnp.concatenate([ref[k : k + 1, j * tokens : (j + 1) * tokens] for j in range(nc)], axis=0)

    own0, own1 = rows_of(r_ref, 0) == e, rows_of(r_ref, 1) == e
    own = own0 | own1
    tick()
    own_pos = dot(own.astype(bf16), before)
    first_slot = (iota((nc, tokens), 1) // SOURCE * CAP).astype(f32)
    goal_ref[...] = jnp.where(own, first_slot + own_pos, -1.0)
    value_ref[...] = jnp.where(own0, rows_of(rw_ref, 0), jnp.where(own1, rows_of(rw_ref, 1), 0.0))

    tick()

    await_bytes(pre.at[pl.ds(0, nz - 1)], s2_recv)
    entering = remote(ent.at[core], ent.at[core], e_send, e_recv, sibling)
    entering.start()
    tick(2)
    await_bytes(ent.at[1 - core], e_recv)
    carried = jnp.concatenate([ent[0], ent[1]], axis=1)
    after0 = (span_sib[...] * carried.astype(f32) + lsib[...].astype(f32)).astype(bf16)
    carried = jnp.where(is0, carried.astype(f32), after0.astype(f32)).astype(bf16)
    tick()
    overall = within + dot(c_ref[...], carried) * jnp.exp(cum_x)
    tick()
    gall[pl.ds(core, 1)] = (overall * silu(gt_ref[...].astype(f32))).astype(bf16)[None]
    both_cores = remote(gall.at[core], gall.at[core], g_send, g_recv, sibling)
    both_cores.start()

    def send_part(part, j):
        @pl.when(j != e)
        def _():
            remote(psend.at[part, j], precv.at[part, e], p_send.at[part], p_recv.at[part], {"exp": j}).start()

    def project(chips, ticks, at_once):
        for k in range(0, len(chips), 2):
            some = chips[k : k + 2]
            out = dot(gall[...].reshape(2 * tokens, width), jnp.concatenate([wbuf[j] for j in some], axis=1)).astype(bf16)
            for s, j in enumerate(some):
                for part in range(2):
                    psend[part, j] = out[part * tokens : (part + 1) * tokens, s * LANES : (s + 1) * LANES]
                send_part(0, j)
                if at_once:
                    send_part(1, j)
            tick(ticks)
        if not at_once:
            for j in chips:
                send_part(1, j)

    def within_reach(apart):
        tick(max(0, len(w_todo) - WQ * (up - apart)))

    def summed(part):
        precv[part, pl.ds(e, 1)] = psend[part, pl.ds(e, 1)]
        await_bytes(psend.at[part, pl.ds(0, ne - 1)], p_recv.at[part])
        total = precv[part, 0].astype(f32)
        for k in range(1, ne):
            total += precv[part, k].astype(f32)
        return total.astype(bf16)

    await_bytes(gall.at[1 - core], g_recv)
    count = 2 * NEAR + 1
    within_reach(NEAR)
    project([ring(z - NEAR + lax.rem(e + k, count)) for k in range(count)], 2, True)
    count = 2 * (MIDDLE - NEAR)
    within_reach(MIDDLE)
    turns = [lax.rem(e + k, count) for k in range(count)]
    project([ring(z + (1 - 2 * (t % 2)) * (NEAR + 1 + t // 2)) for t in turns], 2, True)
    count = nz - 2 * MIDDLE - 1
    within_reach(up)
    project([ring(z + MIDDLE + 1 + lax.rem(e + k, count)) for k in range(count)], 0, False)

    def to_slots(block, values):
        at = pl.ds(pl.multiple_of(block * tokens, tokens), tokens)
        experts = iota((ne, tokens), 0)
        hit = (r_ref[0:1, at] == experts) | (r_ref[1:2, at] == experts)
        pos = dot(hit.astype(bf16), before).astype(jnp.int32)
        target = jnp.where(hit, iota((ne, tokens), 1) // SOURCE * CAP + pos, -1)
        masks = (target[:, None, :] == iota((ne, slots, tokens), 1)).astype(f32).astype(bf16)
        return dot(masks.reshape(ne * slots, tokens), values).astype(bf16).reshape(ne, slots, values.shape[1])

    lane = pl.ds(pl.multiple_of(e * LANES, LANES), LANES)
    dsend[...] = to_slots(z * 2, summed(0))
    for k in range(1, ne):
        j = lax.rem(e + k, ne)
        remote(dsend.at[j], abuf.at[z, core, :, lane], m_send, m_recv, {"exp": j}).start()
    abuf[z, core, :, lane] = dsend[e]

    second_half = summed(1)
    mbuf[0, 0] = second_half
    mbuf[1, 0] = second_half

    def b_ring(i):
        for dd in range(2):
            turn, hops = 1 - 2 * dd, up - dd

            @pl.when((i > 0) & (i <= hops))
            def _():
                await_bytes(mbuf.at[dd, i], b_recv.at[dd, lax.rem(i + up - 1, up)])

            @pl.when(i < hops)
            def _():
                remote(mbuf.at[dd, i], mbuf.at[dd, i + 1], b_send.at[dd], b_recv.at[dd, lax.rem(i, up)], at_z(z + turn)).start()

    def b_dispatch(dd, i):
        chip = ring(z - (1 - 2 * dd) * i)
        bsend[chip] = to_slots(chip * 2 + 1, mbuf[dd, i])

        def one(k, _):
            j = lax.rem(e + k, ne)
            remote(bsend.at[chip, j], bbuf.at[chip, core, :, lane], bd_send, bd_recv.at[chip], {"exp": j}).start()
            return 0

        lax.fori_loop(1, ne, one, 0)
        bbuf[chip, core, :, lane] = bsend[chip, e]

    def b_side(dd, i):
        chip = ring(z - (1 - 2 * dd) * i)
        await_bytes(bsend.at[chip, pl.ds(0, ne - 1)], bd_recv.at[chip])
        block = bbuf.at[chip, core]
        remote(block, block, bs_send, bs_recv.at[chip], sibling).start()

    acols = abuf.shape[3] // AQ

    def a_ring(i, q):
        for dd in range(2):
            turn, hops = 1 - 2 * dd, up if (q < AQ // 2) == (dd == 0) else up - 1
            piece = abuf.at[ring(z - turn * i), core, :, pl.ds(q * acols, acols)]

            @pl.when((i > 0) & (i <= hops))
            def _():
                await_bytes(piece, a_recv.at[dd, lax.rem(i + up - 1, up), q])

            @pl.when(i < hops)
            def _():
                remote(piece, piece, a_send, a_recv.at[dd, lax.rem(i, up), q], at_z(z + turn)).start()

    def a_side(dd, i):
        chip = ring(z - (1 - 2 * dd) * i)
        block = abuf.at[chip, core]
        remote(block, block, as_send, as_recv.at[chip], sibling).start()

    def expert(i):
        chips = (ring(z - i), ring(z + lax.rem(i, up)))
        for chip in chips:
            await_bytes(abuf.at[chip, 1 - core], as_recv.at[chip])
            await_bytes(bbuf.at[chip, 1 - core], bs_recv.at[chip])

        product = None
        for p in range(2):
            rows = jnp.concatenate([buf[chip, p] for chip in chips for buf in (abuf, bbuf)], axis=0)
            part = dot(rows, gbuf[p].reshape(rows.shape[1], gbuf.shape[3]))
            product = part if product is None else product + part
        for k, chip in enumerate(chips):
            weights = []
            for s in range(2):
                goal, value = goal_ref[pl.ds(chip * 2 + s, 1), :], value_ref[pl.ds(chip * 2 + s, 1), :]
                at = goal == iota((slots, tokens), 0).astype(f32)
                weights.append(jnp.sum(jnp.where(at, value, 0.0), axis=1, keepdims=True))
            weight = jnp.concatenate(weights, axis=0)
            part = product[k * 2 * slots : (k + 1) * 2 * slots]
            out_ref[0, pl.ds(pl.multiple_of(chip * 2 * slots, 2 * slots), 2 * slots), :] = (weight * silu(part)).astype(bf16)

    def step(i, _):
        b_ring(i)
        a_ring(i - 1, 0)

        @pl.when(i <= up)
        def _():
            b_dispatch(0, i)

        a_ring(i - 1, 1)

        @pl.when(i < up)
        def _():
            b_dispatch(1, i)

        a_ring(i - 1, 2)

        @pl.when((i > 1) & (i <= up + 2))
        def _():
            b_side(0, i - 2)

        @pl.when((i > 2) & (i < up + 2))
        def _():
            b_side(1, i - 2)

        a_ring(i - 1, 3)

        @pl.when(i <= up + 1)
        def _():
            a_side(0, i - 1)

        @pl.when((i > 1) & (i < up + 1))
        def _():
            a_side(1, i - 1)

        @pl.when(i > 3)
        def _():
            expert(i - 3)

        return 0

    b_ring(0)
    b_dispatch(0, 0)
    for load in load_g:
        load.wait()
    await_bytes(dsend.at[pl.ds(0, ne - 1)], m_recv)
    lax.fori_loop(1, up + 4, step, 0)

    own_state.wait_send()
    own_span.wait_send()
    entering.wait_send()
    await_bytes(stb.at[pl.ds(0, nz - 1)], s1_send)
    await_bytes(rd.at[pl.ds(0, nz - 1)], d1_send)
    await_bytes(pre.at[pl.ds(0, nz - 1)], s2_send)
    await_bytes(wbuf.at[pl.ds(0, nz - 1)], w_send)
    both_cores.wait_send()
    for part in range(2):
        await_bytes(psend.at[part, pl.ds(0, ne - 1)], p_send.at[part])
    await_bytes(dsend.at[pl.ds(0, ne - 1)], m_send)
    await_bytes(abuf.at[pl.ds(0, nz - 1), 0], a_send)
    await_bytes(abuf.at[:, 0], as_send)
    for dd in range(2):
        await_bytes(mbuf.at[dd, pl.ds(0, up - dd)], b_send.at[dd])
    await_bytes(bsend.at[:, pl.ds(0, ne - 1)], bd_send)
    await_bytes(bbuf.at[:, 0], bs_send)


def body(x, gt, b, c, ld, skip, w, routes, weights, gate):
    nc, ne = lax.axis_size("ctx"), lax.axis_size("exp")
    nz = nc // 2
    tokens, width = x.shape
    heads = ld.shape[1]
    depth, shard = w.shape
    wide = shard * nc
    slots = tokens // SOURCE * CAP
    ff = gate.shape[2]
    blocks = width // 2 // LANES
    hbm = pl.BlockSpec(memory_space=pl.ANY)
    dma = pltpu.SemaphoreType.DMA
    r = routes.T
    rw = weights.T

    def vmem(shape, kind=bf16):
        return pltpu.VMEM(shape, kind)

    return pl.pallas_call(
        kernel,
        out_shape=jax.ShapeDtypeStruct((1, nc * slots, ff), bf16),
        in_specs=[hbm] * 8 + [pl.BlockSpec(memory_space=pltpu.VMEM), hbm],
        out_specs=pl.BlockSpec(memory_space=pltpu.VMEM),
        scratch_shapes=[
            vmem(x.shape), vmem(gt.shape), vmem(b.shape), vmem(c.shape), vmem((heads, tokens), f32), vmem((1, heads), f32),
            vmem(r.shape, jnp.int32), vmem(rw.shape, f32),
            vmem((2, ne, LANES, ff)), vmem((nz, depth, shard)),
            vmem((nz, 2, slots, wide // 2)), vmem((nz, 2, slots, wide // 2)),
            vmem((2, ne, tokens, LANES)), vmem((2, ne, tokens, LANES)),
            vmem((ne, slots, LANES)), vmem((nz, ne, slots, LANES)), vmem((2, nz // 2 + 1, tokens, LANES)),
            vmem((2, *x.shape)), vmem((b.shape[1], width)), vmem((b.shape[1], width)), vmem((1, width), f32), vmem((1, width), f32),
            vmem((nz, 16, LANES)), vmem((blocks, 1, LANES), f32), vmem((nz, 16, LANES)), vmem((nz, 1, LANES), f32),
            vmem((nz, 16, LANES)), vmem((2, b.shape[1], width // 2)),
            vmem((nc, tokens), f32), vmem((nc, tokens), f32),
            dma((10,)), dma((2,)), dma((2,)), dma, dma, dma, dma, dma, dma, dma, dma,
            dma, dma((2, nz // 2, WQ)), dma, dma,
            dma((2,)), dma((2,)), dma, dma,
            dma, dma((2, nz // 2, AQ)), dma, dma((nz,)),
            dma((2,)), dma((2, nz // 2)), dma, dma((nz,)), dma, dma((nz,)),
        ],
        compiler_params=pltpu.CompilerParams(
            collective_id=0, has_side_effects=True, vmem_limit_bytes=56 * 2**20
        ),
        name="hybrid_block",
    )(x, gt, b, c, ld.T, skip.reshape(1, heads), w, r, rw, gate.reshape(ne, 2, LANES, ff))


def solution(mesh):
    in_specs = (
        P("ctx", "exp"),
        P("ctx", "exp"),
        P("ctx", None),
        P("ctx", None),
        P("ctx", "exp"),
        P("exp"),
        P("exp", "ctx"),
        P(),
        P(),
        P("exp", None, "ctx"),
    )
    out_specs = P("exp", None, "ctx")
    return jax.shard_map(body, mesh=mesh, in_specs=in_specs, out_specs=out_specs, check_vma=False)
```
